32 devices in a mesh: dp: 4 (over z), ctx: 8 (over y, x, core).
Axes of the slice: x: 2, y: 2, z: 4, core: 2. Of those that a mesh axis runs over, the one named last changes fastest.
Arguments:
- gate_in: bfloat16 [4, 2048, 2048], P('dp', 'ctx'), may hold values from -6 to 6
- values: bfloat16 [4, 2048, 2048], P('dp', 'ctx'), may hold values from -6 to 6
- gate_out: bfloat16 [4, 2048, 2048], P('dp', 'ctx'), may hold values from -6 to 6
- cotangent: bfloat16 [4, 2048, 2048], P('dp', 'ctx'), may hold values from -6 to 6
- filters: bfloat16 [2048, 2048], P(None, 'ctx'), may hold values from -6 to 6
- skip_gain: float32 [2048], replicated, may hold values from -3 to 3
Outputs:
- grad_gate_in: bfloat16 [4, 2048, 2048], P('dp', 'ctx')
- grad_values: bfloat16 [4, 2048, 2048], P('dp', 'ctx')
- grad_gate_out: bfloat16 [4, 2048, 2048], P('dp', 'ctx')
- grad_filters: float32 [2048, 2048], P('dp', 'ctx')
The draws below stay inside these ranges and needn't reach their ends.
All inputs are finite; a program needn't handle non-finite values.
Results may differ from the reference program's by a relative error of at most 0.014.
Values may be sent and summed in bfloat16 or wider, within the bound.
A program may use at most 128 MiB of HBM per device.

```python
import math
import jax
import jax.numpy as jnp
from jax import lax

D = 2048
RADIX = 128
L = 2048
NFFT = 4096
N1 = 32
SEQS = 4
N_CTX = 8


def block_levels(own_key, dims, cuts, low, high):
    factor_of = 1.0
    for dim, blocks in cuts:
        draws = jax.random.uniform(jax.random.fold_in(jax.random.fold_in(own_key, 6), dim), (blocks,), jnp.float32, low / len(cuts), high / len(cuts))
        factor_of = factor_of * jnp.repeat(jnp.exp(draws), dims[dim] // blocks).reshape((-1,) + (1,) * (len(dims) - 1 - dim))
    return factor_of


def normal_values(own_key, shape, width, bound, split=(), kind=jnp.bfloat16):
    values = width * jax.random.normal(own_key, shape, jnp.float32)
    if split:
        values = values * block_levels(own_key, shape, split, -0.22, 0.18)
    return jnp.clip(values, -bound, bound).astype(kind)


def setup_inputs(seed: int = 0) -> dict:
    key_list = jax.random.split(jax.random.key(seed), 7)
    gate_in = normal_values(key_list[0], (SEQS, L, D), 1.0, 6.0, ((0, 4), (1, 8)))
    values = normal_values(key_list[1], (SEQS, L, D), 1.0, 6.0, ((0, 4), (1, 8)))
    gate_out = normal_values(key_list[2], (SEQS, L, D), 1.0, 6.0, ((0, 4), (1, 8)))
    cotangent = normal_values(key_list[3], (SEQS, L, D), 1.0, 6.0, ((0, 4), (1, 8)))
    filters = normal_values(key_list[4], (L, D), 1.0, 6.0, ((1, 8),))
    skip_gain = normal_values(key_list[5], (D,), 0.5, 3.0, (), jnp.float32)
    return dict(gate_in=gate_in, values=values, gate_out=gate_out, cotangent=cotangent, filters=filters, skip_gain=skip_gain)


def counting(count):
    return jnp.arange(count, dtype=jnp.int32)


def phase_pair(row_index, col_index, period, sign_value):
    product = (row_index[:, None] * col_index[None, :]) % period
    phases = product.astype(jnp.float32) * (2.0 * math.pi / period)
    return jnp.cos(phases), sign_value * jnp.sin(phases)


def contract(form, left, right):
    return jnp.einsum(form, left.astype(jnp.float32), right.astype(jnp.float32))


def radix_table(sign_value):
    cos_r, sin_r = phase_pair(counting(RADIX), counting(RADIX), RADIX, sign_value)
    return jnp.stack([jnp.stack([cos_r, sin_r], 1), jnp.stack([-sin_r, cos_r], 1)]).astype(jnp.bfloat16)


def forward_transform(signal):
    length, channels = signal.shape
    half_rows = length // RADIX
    outer_rows = 2 * half_rows
    fft_size = 2 * length
    cos_a, sin_a = phase_pair(counting(outer_rows), counting(half_rows), outer_rows, -1.0)
    table_a = jnp.stack([cos_a, sin_a]).astype(jnp.bfloat16)
    section_one = contract("pka,abc->pkbc", table_a, signal.reshape(half_rows, RADIX, channels))
    cos_t, sin_t = phase_pair(counting(outer_rows), counting(RADIX), fft_size, -1.0)
    real_part = section_one[0] * cos_t[:, :, None] - section_one[1] * sin_t[:, :, None]
    imag_part = section_one[0] * sin_t[:, :, None] + section_one[1] * cos_t[:, :, None]
    twisted = jnp.stack([real_part, imag_part]).astype(jnp.bfloat16)
    return contract("pkbc,pbqm->qkmc", twisted, radix_table(-1.0)).astype(jnp.bfloat16)


def inverse_prep(spectrum, k_start, outer_rows):
    fft_size = outer_rows * RADIX
    mixed = contract("pkmc,pmqb->qkbc", spectrum, radix_table(1.0))
    k_rows = k_start + counting(spectrum.shape[1])
    cos_t, sin_t = phase_pair(k_rows, counting(RADIX), fft_size, 1.0)
    real_part = mixed[0] * cos_t[:, :, None] - mixed[1] * sin_t[:, :, None]
    imag_part = mixed[0] * sin_t[:, :, None] + mixed[1] * cos_t[:, :, None]
    return jnp.stack([real_part, imag_part]).astype(jnp.bfloat16)


def inverse_rows(twisted, k_start, row_start, row_count, outer_rows, scale_out):
    k_rows = k_start + counting(twisted.shape[1])
    a_rows = row_start + counting(row_count)
    cos_e, sin_e = phase_pair(k_rows, a_rows, outer_rows, 1.0)
    table_e = jnp.stack([cos_e, -sin_e]).astype(jnp.bfloat16)
    result = contract("pka,pkbc->abc", table_e, twisted) * scale_out
    return result.reshape(row_count * RADIX, twisted.shape[3])


def spectral_product(left, right, conj_left):
    left_re = left[0].astype(jnp.float32)
    left_im = left[1].astype(jnp.float32)
    right_re = right[0].astype(jnp.float32)
    right_im = right[1].astype(jnp.float32)
    if conj_left:
        return jnp.stack([left_re * right_re + left_im * right_im, left_re * right_im - left_im * right_re])
    return jnp.stack([left_re * right_re - left_im * right_im, left_re * right_im + left_im * right_re])


def reference(gate_in, values, gate_out, cotangent, filters, skip_gain):
    channels = D // N_CTX
    scale_out = L ** -0.5 / NFFT

    def block(block_index):
        start = block_index * channels

        def take(array):
            return lax.dynamic_slice_in_dim(array, start, channels, axis=array.ndim - 1)

        gain = take(skip_gain)[None, :]
        spec_filter = forward_transform(take(filters))
        grad_filter = jnp.zeros((L, channels), jnp.float32)
        list_in, list_val, list_out = [], [], []
        for seq_index in range(SEQS):
            gin = take(gate_in[seq_index]).astype(jnp.float32)
            vals = take(values[seq_index]).astype(jnp.float32)
            gout = take(gate_out[seq_index]).astype(jnp.float32)
            cots = take(cotangent[seq_index]).astype(jnp.float32)
            gated = (gin * vals).astype(jnp.bfloat16)
            conv_grad = (cots * gout).astype(jnp.bfloat16)
            spec_gated = forward_transform(gated)
            spec_grad = forward_transform(conv_grad)
            conv_prod = spectral_product(spec_filter, spec_gated, False).astype(jnp.bfloat16)
            back_prod = spectral_product(spec_filter, spec_grad, True).astype(jnp.bfloat16)
            conv = inverse_rows(inverse_prep(conv_prod, 0, N1), 0, 0, N1 // 2, N1, scale_out).astype(jnp.bfloat16)
            back = inverse_rows(inverse_prep(back_prod, 0, N1), 0, 0, N1 // 2, N1, scale_out).astype(jnp.bfloat16)
            gated_f = gated.astype(jnp.float32)
            list_out.append((cots * (conv.astype(jnp.float32) + gain * gated_f)).astype(jnp.bfloat16))
            grad_gated = back.astype(jnp.float32) + gain * conv_grad.astype(jnp.float32)
            list_in.append((grad_gated * vals).astype(jnp.bfloat16))
            list_val.append((grad_gated * gin).astype(jnp.bfloat16))
            cross = spectral_product(spec_gated, spec_grad, True).astype(jnp.bfloat16)
            grad_filter = grad_filter + inverse_rows(inverse_prep(cross, 0, N1), 0, 0, N1 // 2, N1, scale_out)
        return jnp.stack(list_in), jnp.stack(list_val), jnp.stack(list_out), grad_filter

    res_in, res_val, res_out, res_filter = lax.map(block, jnp.arange(N_CTX, dtype=jnp.int32))

    def arrange(stacked):
        return jnp.transpose(stacked, (1, 2, 0, 3)).reshape(SEQS, L, D)

    grad_filters = jnp.transpose(res_filter, (1, 0, 2)).reshape(L, D)
    return arrange(res_in), arrange(res_val), arrange(res_out), grad_filters
```

```python
import functools
import math

import jax
import jax.numpy as jnp
import ml_dtypes
import numpy as np
from jax import lax
from jax.experimental import pallas as pl
from jax.experimental.pallas import tpu as pltpu
from jax.sharding import PartitionSpec as P

RADIX = 128
GROUP = 16
BF16 = jnp.bfloat16
F32 = jnp.float32


def make_tables(length):
    half = length // RADIX
    size = 2 * length
    scale = length ** (-0.5) / size
    groups = RADIX // GROUP
    a = np.arange(half)
    b = np.arange(RADIX)
    j = np.arange(half)
    pos = 128 * a[None, :] + b[:, None]
    ang = 2 * math.pi * ((pos[:, None, :] * j[None, :, None]) % size) / size
    first = np.stack([np.cos(ang), -np.sin(ang)], 2)
    first[:, 0, 0, :] = 1.0
    first[:, 0, 1, :] = (-1.0) ** a[None, :]
    last = first * np.where(j == 0, scale, 2 * scale)[None, :, None, None]
    first = first.reshape(groups, GROUP, half, 2, half)
    last = last.reshape(groups, GROUP, half, 2, half)
    eye = np.eye(GROUP)
    table_a = np.einsum("gijpa,ik->gjpiak", first, eye).reshape(
        groups, half * 2 * GROUP, half * GROUP
    )
    table_e = np.einsum("gijpa,ik->gaijpk", last, eye).reshape(
        groups, half * GROUP, half * 2 * GROUP
    )
    ang = 2 * math.pi * (np.outer(b, b) % RADIX) / RADIX
    cos, sin = np.cos(ang), np.sin(ang)
    general = np.block([[cos, sin], [-sin, cos]])
    inverse = np.block([[cos, -sin], [sin, cos]])
    hr = RADIX // 2
    packed = np.zeros((2, RADIX, 2, RADIX))
    packed_inv = np.zeros((2, RADIX, 2, RADIX))
    s = np.arange(hr)
    ang0 = 2 * math.pi * (np.outer(s, b) % RADIX) / RADIX
    packed[0, :hr, 0] = np.cos(ang0)
    packed[1, :hr, 0] = -np.sin(ang0)
    packed[1, 0, 0] = (-1.0) ** b
    ang1 = 2 * math.pi * (np.outer(2 * s + 1, b) % (2 * RADIX)) / (2 * RADIX)
    packed[0, hr:, 1] = np.cos(ang1)
    packed[1, hr:, 1] = -np.sin(ang1)
    packed_inv = 2.0 * np.transpose(packed, (2, 3, 0, 1))
    packed_inv[0, :, 0, 0] = 1.0
    packed_inv[0, :, 1, 0] = (-1.0) ** b
    full = 2 * RADIX
    table_b = np.stack([packed.reshape(full, full), general])
    table_c = np.stack([packed_inv.reshape(full, full), inverse])
    return tuple(t.astype(ml_dtypes.bfloat16) for t in (table_a, table_b, table_c, table_e))


def dot(left, right):
    return jnp.dot(left, right, preferred_element_type=F32)


def partner(me, step, count):
    if count & (count - 1):
        return lax.rem(me + step, count)
    peer = me
    bit = 1
    while bit < count:
        if step & bit:
            peer = peer + bit * (1 - 2 * ((me // bit) % 2))
        bit *= 2
    return peer


def send_order(count):
    return sorted(range(1, count), key=lambda k: (-(k // 2).bit_count(), k))


def spectral_product(left, right, conj_left, packed):
    lr = left[:RADIX].astype(F32)
    li = left[RADIX:].astype(F32)
    rr = right[:RADIX].astype(F32)
    ri = right[RADIX:].astype(F32)
    real_real = lr * rr
    imag_imag = li * ri
    if conj_left:
        real = real_real + imag_imag
        imag = lr * ri - li * rr
    else:
        real = real_real - imag_imag
        imag = lr * ri + li * rr
    if packed:
        first = lax.broadcasted_iota(jnp.int32, lr.shape, 0) == 0
        real = jnp.where(first, real_real, real)
        imag = jnp.where(first, imag_imag, imag)
    return jnp.concatenate([real, imag], 0).astype(BF16)


def kernel(
    n_ctx,
    n_dp,
    gin_h,
    val_h,
    gout_h,
    cot_h,
    filt_h,
    ta_h,
    tb_h,
    tc_h,
    te_h,
    conv_out,
    back_out,
    part_out,
    gin,
    val,
    gout,
    cot,
    filt,
    ta,
    tb,
    tc,
    te,
    gated,
    cgrad,
    gated_ch,
    cgrad_ch,
    mid,
    spec_f,
    spec_g,
    mixed,
    mixed_x,
    conv_ch,
    back_ch,
    own_ch,
    load_sem,
    own_sem,
    send_sem,
    recv_sem,
    dp_send,
    dp_recv,
):
    me = lax.axis_index("ctx")
    seq = lax.axis_index("dp")
    tok, _ = gin.shape
    length, chans = filt.shape
    half = length // RADIX
    groups = RADIX // GROUP
    piece = length // n_dp

    barrier = pltpu.get_barrier_semaphore()
    for k in range(1, n_ctx):
        pl.semaphore_signal(barrier, inc=1, device_id={"ctx": partner(me, k, n_ctx)})
    for k in range(1, n_dp):
        pl.semaphore_signal(barrier, inc=1, device_id={"dp": partner(seq, k, n_dp)})

    loads = []
    for i, (src, dst) in enumerate(
        [
            (gin_h, gin),
            (val_h, val),
            (cot_h, cot),
            (gout_h, gout),
            (filt_h, filt),
            (ta_h, ta),
            (tb_h, tb),
            (tc_h, tc),
            (te_h, te),
        ]
    ):
        copy = pltpu.make_async_copy(src, dst, load_sem.at[i])
        copy.start()
        loads.append(copy)

    def columns(index):
        return pl.ds(pl.multiple_of(index * chans, chans), chans)

    def rows(index, count):
        return pl.ds(pl.multiple_of(index * count, count), count)

    def forward_sends(which, left, right, staged, landed):
        copies = []
        for k in send_order(n_ctx):
            peer = partner(me, k, n_ctx)
            block = left[:, columns(peer)].astype(F32) * right[:, columns(peer)].astype(F32)
            staged[:, columns(peer)] = block.astype(BF16)
            copy = pltpu.make_async_remote_copy(
                src_ref=staged.at[:, columns(peer)],
                dst_ref=landed.at[rows(me, tok), :],
                send_sem=send_sem.at[which, k],
                recv_sem=recv_sem.at[which, k],
                device_id={"ctx": peer},
            )
            copy.start()
            copies.append(copy)
        block = left[:, columns(me)].astype(F32) * right[:, columns(me)].astype(F32)
        landed[rows(me, tok), :] = block.astype(BF16)
        return copies

    def return_sends(which, source, target):
        copies = []
        for k in send_order(n_ctx):
            peer = partner(me, k, n_ctx)
            copy = pltpu.make_async_remote_copy(
                src_ref=source.at[rows(peer, tok), :],
                dst_ref=target.at[:, columns(me)],
                send_sem=send_sem.at[which, k],
                recv_sem=recv_sem.at[which, k],
                device_id={"ctx": peer},
            )
            copy.start()
            copies.append(copy)
        own = pltpu.make_async_copy(
            source.at[rows(me, tok), :], target.at[:, columns(me)], own_sem.at[which - 2]
        )
        own.start()
        return copies, own

    def first_stage(source):
        def body(g, carry):
            part = [source[pl.ds(pl.multiple_of(a * RADIX + g * GROUP, GROUP), GROUP), :]
                    for a in range(half)]
            out = dot(ta[g], jnp.concatenate(part, 0)).astype(BF16)
            for row in range(2 * half):
                mid[pl.ds(pl.multiple_of(row * RADIX + g * GROUP, GROUP), GROUP), :] = out[
                    row * GROUP : (row + 1) * GROUP
                ]
            return carry

        lax.fori_loop(0, groups, body, 0)

    def last_stage(source, target):
        def body(g, carry):
            part = [source[pl.ds(pl.multiple_of(row * RADIX + g * GROUP, GROUP), GROUP), :]
                    for row in range(2 * half)]
            out = dot(te[g], jnp.concatenate(part, 0)).astype(BF16)
            for a in range(half):
                target[pl.ds(pl.multiple_of(a * RADIX + g * GROUP, GROUP), GROUP), :] = out[
                    a * GROUP : (a + 1) * GROUP
                ]
            return carry

        lax.fori_loop(0, groups, body, 0)

    def each_row(step):
        step(0, True)

        def body(j, carry):
            step(j, False)
            return carry

        lax.fori_loop(1, half, body, 0)

    def spectrum(j, packed):
        table = tb[0 if packed else 1]
        return dot(table, mid[rows(j, 2 * RADIX), :]).astype(BF16)

    def unmix(target, j, packed, product):
        table = tc[0 if packed else 1]
        target[rows(j, 2 * RADIX), :] = dot(table, product).astype(BF16)

    loads[0].wait()
    loads[1].wait()
    pl.semaphore_wait(barrier, n_ctx - 1 + n_dp - 1)
    sent_gated = forward_sends(0, gin, val, gated, gated_ch)
    loads[2].wait()
    loads[3].wait()
    sent_cgrad = forward_sends(1, cot, gout, cgrad, cgrad_ch)

    for copy in loads[4:]:
        copy.wait()
    first_stage(filt)

    def filter_row(j, packed):
        spec_f[rows(j, 2 * RADIX), :] = spectrum(j, packed)

    each_row(filter_row)

    for copy in sent_gated:
        copy.wait_recv()
    first_stage(gated_ch)

    def gated_row(j, packed):
        spec = spectrum(j, packed)
        spec_g[rows(j, 2 * RADIX), :] = spec
        unmix(mixed, j, packed, spectral_product(
            spec_f[rows(j, 2 * RADIX), :], spec, False, packed))

    each_row(gated_row)
    last_stage(mixed, conv_ch)
    sent_conv, own_conv = return_sends(2, conv_ch, conv_out)

    for copy in sent_cgrad:
        copy.wait_recv()
    first_stage(cgrad_ch)

    def cgrad_row(j, packed):
        spec = spectrum(j, packed)
        unmix(mixed_x, j, packed, spectral_product(
            spec_g[rows(j, 2 * RADIX), :], spec, True, packed))
        unmix(mixed, j, packed, spectral_product(
            spec_f[rows(j, 2 * RADIX), :], spec, True, packed))

    each_row(cgrad_row)
    last_stage(mixed_x, own_ch)
    sent_part = []
    for k in range(1, n_dp):
        peer = partner(seq, k, n_dp)
        copy = pltpu.make_async_remote_copy(
            src_ref=own_ch.at[rows(peer, piece), :],
            dst_ref=part_out.at[seq],
            send_sem=dp_send.at[k],
            recv_sem=dp_recv.at[k],
            device_id={"dp": peer},
        )
        copy.start()
        sent_part.append(copy)
    own_part = pltpu.make_async_copy(
        own_ch.at[rows(seq, piece), :], part_out.at[seq], own_sem.at[2]
    )
    own_part.start()
    last_stage(mixed, back_ch)
    sent_back, own_back = return_sends(3, back_ch, back_out)

    for copy in sent_gated + sent_cgrad:
        copy.wait_send()
    own_conv.wait()
    own_back.wait()
    own_part.wait()
    for copy in sent_conv + sent_back + sent_part:
        copy.wait()


def transfer_and_transform(gin, val, gout, cot, filters):
    n_ctx = lax.axis_size("ctx")
    n_dp = lax.axis_size("dp")
    tok, width = gin.shape
    length, chans = filters.shape
    tables = [jnp.asarray(t) for t in make_tables(length)]
    full = 2 * length
    any_spec = pl.BlockSpec(memory_space=pl.ANY)
    outs = (
        jax.ShapeDtypeStruct((tok, width), BF16),
        jax.ShapeDtypeStruct((tok, width), BF16),
        jax.ShapeDtypeStruct((n_dp, length // n_dp, chans), BF16),
    )
    vmem = lambda *shape: pltpu.VMEM(shape, BF16)
    dma = lambda *shape: pltpu.SemaphoreType.DMA(shape)
    return pl.pallas_call(
        functools.partial(kernel, n_ctx, n_dp),
        out_shape=outs,
        in_specs=[any_spec] * 9,
        out_specs=[any_spec] * 3,
        scratch_shapes=[vmem(tok, width)] * 4
        + [vmem(length, chans)]
        + [vmem(*t.shape) for t in tables]
        + [vmem(tok, width)] * 2
        + [vmem(length, chans)] * 2
        + [vmem(full, chans)] * 5
        + [vmem(length, chans)] * 3
        + [dma(9), dma(3), dma(4, n_ctx), dma(4, n_ctx), dma(n_dp), dma(n_dp)],
        compiler_params=pltpu.CompilerParams(
            collective_id=0, has_side_effects=True, vmem_limit_bytes=44 * 2**20
        ),
        cost_estimate=pl.CostEstimate(
            flops=12 * 2 * 512 * 256 * full * chans // 65536,
            bytes_accessed=12 * 2**20,
            transcendentals=0,
        ),
    )(gin, val, gout, cot, filters, *tables)


def on_device(gate_in, values, gate_out, cotangent, filters, skip_gain):
    conv, back, parts = transfer_and_transform(
        gate_in[0], values[0], gate_out[0], cotangent[0], filters
    )
    gin = gate_in[0].astype(F32)
    vals = values[0].astype(F32)
    cots = cotangent[0].astype(F32)
    gated = (gin * vals).astype(BF16).astype(F32)
    conv_grad = (cots * gate_out[0].astype(F32)).astype(BF16).astype(F32)
    gain = skip_gain[None, :]
    grad_gate_out = (cots * (conv.astype(F32) + gain * gated)).astype(BF16)
    grad_gated = back.astype(F32) + gain * conv_grad
    grad_gate_in = (grad_gated * vals).astype(BF16)
    grad_values = (grad_gated * gin).astype(BF16)
    grad_filters = jnp.sum(parts.astype(F32), axis=0)
    return (grad_gate_in[None], grad_values[None], grad_gate_out[None], grad_filters)


def solution(mesh):
    return jax.shard_map(
        on_device,
        mesh=mesh,
        in_specs=(
            P("dp", "ctx", None),
            P("dp", "ctx", None),
            P("dp", "ctx", None),
            P("dp", "ctx", None),
            P(None, "ctx"),
            P(),
        ),
        out_specs=(
            P("dp", "ctx", None),
            P("dp", "ctx", None),
            P("dp", "ctx", None),
            P("dp", "ctx"),
        ),
        check_vma=False,
    )
```

```python
import functools
import math

import jax
import jax.numpy as jnp
import ml_dtypes
import numpy as np
from jax import lax
from jax.experimental import pallas as pl
from jax.experimental.pallas import tpu as pltpu
from jax.sharding import PartitionSpec as P

RADIX = 128
GROUP = 16
BF16 = jnp.bfloat16
F32 = jnp.float32


def make_tables(length):
    half = length // RADIX
    size = 2 * length
    scale = length ** (-0.5) / size
    groups = RADIX // GROUP
    a = np.arange(half)
    b = np.arange(RADIX)
    j = np.arange(half)
    pos = 128 * a[None, :] + b[:, None]
    ang = 2 * math.pi * ((pos[:, None, :] * j[None, :, None]) % size) / size
    first = np.stack([np.cos(ang), -np.sin(ang)], 2)
    first[:, 0, 0, :] = 1.0
    first[:, 0, 1, :] = (-1.0) ** a[None, :]
    last = first * np.where(j == 0, scale, 2 * scale)[None, :, None, None]
    first = first.reshape(groups, GROUP, half, 2, half)
    last = last.reshape(groups, GROUP, half, 2, half)
    eye = np.eye(GROUP)
    table_a = np.einsum("gijpa,ik->gjpiak", first, eye).reshape(
        groups, half * 2 * GROUP, half * GROUP
    )
    table_e = np.einsum("gijpa,ik->gaijpk", last, eye).reshape(
        groups, half * GROUP, half * 2 * GROUP
    )
    ang = 2 * math.pi * (np.outer(b, b) % RADIX) / RADIX
    cos, sin = np.cos(ang), np.sin(ang)
    general = np.block([[cos, sin], [-sin, cos]])
    inverse = np.block([[cos, -sin], [sin, cos]])
    hr = RADIX // 2
    packed = np.zeros((2, RADIX, 2, RADIX))
    packed_inv = np.zeros((2, RADIX, 2, RADIX))
    s = np.arange(hr)
    ang0 = 2 * math.pi * (np.outer(s, b) % RADIX) / RADIX
    packed[0, :hr, 0] = np.cos(ang0)
    packed[1, :hr, 0] = -np.sin(ang0)
    packed[1, 0, 0] = (-1.0) ** b
    ang1 = 2 * math.pi * (np.outer(2 * s + 1, b) % (2 * RADIX)) / (2 * RADIX)
    packed[0, hr:, 1] = np.cos(ang1)
    packed[1, hr:, 1] = -np.sin(ang1)
    packed_inv = 2.0 * np.transpose(packed, (2, 3, 0, 1))
    packed_inv[0, :, 0, 0] = 1.0
    packed_inv[0, :, 1, 0] = (-1.0) ** b
    full = 2 * RADIX
    table_b = np.stack([packed.reshape(full, full), general])
    table_c = np.stack([packed_inv.reshape(full, full), inverse])
    return tuple(t.astype(ml_dtypes.bfloat16) for t in (table_a, table_b, table_c, table_e))


def dot(left, right):
    return jnp.dot(left, right, preferred_element_type=F32)


def partner(me, step, count):
    if count & (count - 1):
        return lax.rem(me + step, count)
    peer = me
    bit = 1
    while bit < count:
        if step & bit:
            peer = peer + bit * (1 - 2 * ((me // bit) % 2))
        bit *= 2
    return peer


def send_order(count):
    return sorted(range(1, count), key=lambda k: (-(k // 2).bit_count(), k))


def spectral_product(left, right, conj_left, packed):
    lr = left[:RADIX].astype(F32)
    li = left[RADIX:].astype(F32)
    rr = right[:RADIX].astype(F32)
    ri = right[RADIX:].astype(F32)
    real_real = lr * rr
    imag_imag = li * ri
    if conj_left:
        real = real_real + imag_imag
        imag = lr * ri - li * rr
    else:
        real = real_real - imag_imag
        imag = lr * ri + li * rr
    if packed:
        first = lax.broadcasted_iota(jnp.int32, lr.shape, 0) == 0
        real = jnp.where(first, real_real, real)
        imag = jnp.where(first, imag_imag, imag)
    return jnp.concatenate([real, imag], 0).astype(BF16)


def kernel(
    n_ctx,
    n_dp,
    gin_h,
    val_h,
    gout_h,
    cot_h,
    filt_h,
    ta_h,
    tb_h,
    tc_h,
    te_h,
    conv_out,
    back_out,
    part_out,
    gin,
    val,
    gout,
    cot,
    filt,
    ta,
    tb,
    tc,
    te,
    mid,
    spec_f,
    mixed,
    mixed_x,
    *rest,
):
    me = lax.axis_index("ctx")
    seq = lax.axis_index("dp")
    tok, _ = gin.shape
    length, chans = filt.shape
    halves = max(1, chans // 128)
    lanes = chans // halves
    half = length // RADIX
    groups = RADIX // GROUP
    piece = length // n_dp
    staged, landed, ret, own = (rest[i * halves : (i + 1) * halves] for i in range(4))
    load_sem, own_sem, send_sem, recv_sem, dp_send, dp_recv = rest[4 * halves :]

    barrier = pltpu.get_barrier_semaphore()
    for k in range(1, n_ctx):
        pl.semaphore_signal(barrier, inc=1, device_id={"ctx": partner(me, k, n_ctx)})
    for k in range(1, n_dp):
        pl.semaphore_signal(barrier, inc=1, device_id={"dp": partner(seq, k, n_dp)})

    loads = []
    for i, (src, dst) in enumerate(
        [
            (gin_h, gin),
            (val_h, val),
            (cot_h, cot),
            (gout_h, gout),
            (filt_h, filt),
            (ta_h, ta),
            (tb_h, tb),
            (tc_h, tc),
            (te_h, te),
        ]
    ):
        copy = pltpu.make_async_copy(src, dst, load_sem.at[i])
        copy.start()
        loads.append(copy)

    def span(start, count, unit):
        return pl.ds(pl.multiple_of(start, unit), count)

    def pair(index):
        return span(index * 2 * lanes, 2 * lanes, 2 * lanes)

    def rows(index, count):
        return span(index * count, count, count)

    def gate(h, index, target, where):
        cols = span(index * chans + h * lanes, lanes, lanes)
        block = gin[:, cols].astype(F32) * val[:, cols].astype(F32)
        grad = cot[:, cols].astype(F32) * gout[:, cols].astype(F32)
        target[where] = jnp.concatenate([block, grad], 1).astype(BF16)

    def forward_sends(h):
        copies = []
        for k in send_order(n_ctx):
            peer = partner(me, k, n_ctx)
            gate(h, peer, staged[h], (slice(None), pair(peer)))
            copy = pltpu.make_async_remote_copy(
                src_ref=staged[h].at[:, pair(peer)],
                dst_ref=landed[h].at[rows(me, tok), :],
                send_sem=send_sem.at[h, k],
                recv_sem=recv_sem.at[h, k],
                device_id={"ctx": peer},
            )
            copy.start()
            copies.append(copy)
        gate(h, me, landed[h], (rows(me, tok), slice(None)))
        return copies

    def return_sends(h):
        copies = []
        here = []
        for t, target in enumerate((conv_out, back_out)):
            dst = target.at[:, span(me * chans + h * lanes, lanes, lanes)]
            cols = pl.ds(t * lanes, lanes)
            for k in send_order(n_ctx):
                peer = partner(me, k, n_ctx)
                copy = pltpu.make_async_remote_copy(
                    src_ref=ret[h].at[rows(peer, tok), cols],
                    dst_ref=dst,
                    send_sem=send_sem.at[halves + 2 * h + t, k],
                    recv_sem=recv_sem.at[halves + 2 * h + t, k],
                    device_id={"ctx": peer},
                )
                copy.start()
                copies.append(copy)
            copy = pltpu.make_async_copy(
                ret[h].at[rows(me, tok), cols], dst, own_sem.at[2 * h + t]
            )
            copy.start()
            here.append(copy)
        return copies, here

    def part_sends(h):
        copies = []
        cols = pl.ds(h * lanes, lanes)
        for k in range(1, n_dp):
            peer = partner(seq, k, n_dp)
            copy = pltpu.make_async_remote_copy(
                src_ref=own[h].at[rows(peer, piece), :],
                dst_ref=part_out.at[seq, :, cols],
                send_sem=dp_send.at[h, k],
                recv_sem=dp_recv.at[h, k],
                device_id={"dp": peer},
            )
            copy.start()
            copies.append(copy)
        here = pltpu.make_async_copy(
            own[h].at[rows(seq, piece), :], part_out.at[seq, :, cols], own_sem.at[2 * halves + h]
        )
        here.start()
        return copies, [here]

    def repeat(first, count, most, step):
        width = max(w for w in range(1, most + 1) if count % w == 0)

        def body(i, carry):
            stores = [step(first + i * width + u) for u in range(width)]
            for store in stores:
                store()
            return carry

        lax.fori_loop(0, count // width, body, 0)

    def first_stage(source):
        def step(g):
            part = [source[span(a * RADIX + g * GROUP, GROUP, GROUP), :] for a in range(half)]
            out = dot(ta[g], jnp.concatenate(part, 0)).astype(BF16)

            def store():
                for row in range(2 * half):
                    mid[span(row * RADIX + g * GROUP, GROUP, GROUP), : out.shape[1]] = out[
                        row * GROUP : (row + 1) * GROUP
                    ]

            return store

        repeat(0, groups, 4, step)

    def last_stage(source, target):
        def step(g):
            part = [
                source[span(row * RADIX + g * GROUP, GROUP, GROUP), :] for row in range(2 * half)
            ]
            out = dot(te[g], jnp.concatenate(part, 0)).astype(BF16)

            def store():
                for a in range(half):
                    target[span(a * RADIX + g * GROUP, GROUP, GROUP), :] = out[
                        a * GROUP : (a + 1) * GROUP
                    ]

            return store

        repeat(0, groups, 4, step)

    def filter_row(j, packed):
        where = rows(j, 2 * RADIX)
        spec = dot(tb[0 if packed else 1], mid[where, :chans]).astype(BF16)

        def store():
            spec_f[where, :] = spec

        return store

    def half_row(h, j, packed):
        where = rows(j, 2 * RADIX)
        which = 0 if packed else 1
        spec = dot(tb[which], mid[where, :]).astype(BF16)
        spec_g, spec_c = spec[:, :lanes], spec[:, lanes:]
        filt_row = spec_f[where, h * lanes : (h + 1) * lanes]
        cross = spectral_product(spec_g, spec_c, True, packed)
        both = jnp.concatenate(
            [
                spectral_product(filt_row, spec_g, False, packed),
                spectral_product(filt_row, spec_c, True, packed),
            ],
            1,
        )
        out_x = dot(tc[which], cross).astype(BF16)
        out = dot(tc[which], both).astype(BF16)

        def store():
            mixed_x[where, :] = out_x
            mixed[where, :] = out

        return store

    def each_row(step):
        step(0, True)()
        repeat(1, half - 1, 5, lambda j: step(j, False))

    for copy in loads[:4]:
        copy.wait()
    pl.semaphore_wait(barrier, n_ctx - 1 + n_dp - 1)
    sent = [forward_sends(h) for h in range(halves)]

    for copy in loads[4:]:
        copy.wait()
    first_stage(filt)
    each_row(filter_row)

    remote = []
    local = []
    for h in range(halves):
        for copy in sent[h]:
            copy.wait_recv()
        first_stage(landed[h])
        each_row(functools.partial(half_row, h))
        last_stage(mixed_x, own[h])
        copies, here = part_sends(h)
        remote += copies
        local += here
        last_stage(mixed, ret[h])
        copies, here = return_sends(h)
        remote += copies
        local += here

    for copy in sum(sent, []):
        copy.wait_send()
    for copy in local + remote:
        copy.wait()


def transfer_and_transform(gin, val, gout, cot, filters):
    n_ctx = lax.axis_size("ctx")
    n_dp = lax.axis_size("dp")
    tok, width = gin.shape
    length, chans = filters.shape
    tables = [jnp.asarray(t) for t in make_tables(length)]
    full = 2 * length
    halves = max(1, chans // 128)
    lanes = chans // halves
    pair = 2 * lanes
    outs = (
        jax.ShapeDtypeStruct((tok, width), BF16),
        jax.ShapeDtypeStruct((tok, width), BF16),
        jax.ShapeDtypeStruct((n_dp, length // n_dp, chans), BF16),
    )
    vmem = lambda *shape: pltpu.VMEM(shape, BF16)
    dma = lambda *shape: pltpu.SemaphoreType.DMA(shape)
    return pl.pallas_call(
        functools.partial(kernel, n_ctx, n_dp),
        out_shape=outs,
        in_specs=[pl.BlockSpec(memory_space=pltpu.HBM)] * 9,
        out_specs=[pl.BlockSpec(memory_space=pl.ANY)] * 3,
        scratch_shapes=[vmem(tok, width)] * 4
        + [vmem(length, chans)]
        + [vmem(*t.shape) for t in tables]
        + [vmem(full, pair), vmem(full, chans), vmem(full, pair), vmem(full, lanes)]
        + [vmem(tok, n_ctx * pair)] * halves
        + [vmem(length, pair)] * halves
        + [vmem(length, pair)] * halves
        + [vmem(length, lanes)] * halves
        + [dma(9), dma(3 * halves), dma(3 * halves, n_ctx), dma(3 * halves, n_ctx)]
        + [dma(halves, n_dp), dma(halves, n_dp)],
        compiler_params=pltpu.CompilerParams(
            collective_id=0, has_side_effects=True, vmem_limit_bytes=56 * 2**20
        ),
        cost_estimate=pl.CostEstimate(
            flops=12 * 2 * 512 * 256 * full * chans // 65536,
            bytes_accessed=12 * 2**20,
            transcendentals=0,
        ),
    )(gin, val, gout, cot, filters, *tables)


def on_device(gate_in, values, gate_out, cotangent, filters, skip_gain):
    conv, back, parts = transfer_and_transform(
        gate_in[0], values[0], gate_out[0], cotangent[0], filters
    )
    gin = gate_in[0].astype(F32)
    vals = values[0].astype(F32)
    cots = cotangent[0].astype(F32)
    gated = (gin * vals).astype(BF16).astype(F32)
    conv_grad = (cots * gate_out[0].astype(F32)).astype(BF16).astype(F32)
    gain = skip_gain[None, :]
    grad_gate_out = (cots * (conv.astype(F32) + gain * gated)).astype(BF16)
    grad_gated = back.astype(F32) + gain * conv_grad
    grad_gate_in = (grad_gated * vals).astype(BF16)
    grad_values = (grad_gated * gin).astype(BF16)
    grad_filters = jnp.sum(parts.astype(F32), axis=0)
    return (grad_gate_in[None], grad_values[None], grad_gate_out[None], grad_filters)


def solution(mesh):
    return jax.shard_map(
        on_device,
        mesh=mesh,
        in_specs=(
            P("dp", "ctx", None),
            P("dp", "ctx", None),
            P("dp", "ctx", None),
            P("dp", "ctx", None),
            P(None, "ctx"),
            P(),
        ),
        out_specs=(
            P("dp", "ctx", None),
            P("dp", "ctx", None),
            P("dp", "ctx", None),
            P("dp", "ctx"),
        ),
        check_vma=False,
    )
```

```python
import functools
import math

import jax
import jax.numpy as jnp
import ml_dtypes
import numpy as np
from jax import lax
from jax.experimental import pallas as pl
from jax.experimental.pallas import tpu as pltpu
from jax.sharding import PartitionSpec as P

RADIX = 128
GROUP = 16
BF16 = jnp.bfloat16
F32 = jnp.float32


def make_tables(length):
    half = length // RADIX
    size = 2 * length
    scale = length ** (-0.5) / size
    groups = RADIX // GROUP
    a = np.arange(half)
    b = np.arange(RADIX)
    j = np.arange(half)
    pos = 128 * a[None, :] + b[:, None]
    ang = 2 * math.pi * ((pos[:, None, :] * j[None, :, None]) % size) / size
    first = np.stack([np.cos(ang), -np.sin(ang)], 2)
    first[:, 0, 0, :] = 1.0
    first[:, 0, 1, :] = (-1.0) ** a[None, :]
    last = first * np.where(j == 0, scale, 2 * scale)[None, :, None, None]
    first = first.reshape(groups, GROUP, half, 2, half)
    last = last.reshape(groups, GROUP, half, 2, half)
    eye = np.eye(GROUP)
    table_a = np.einsum("gijpa,ik->gjpiak", first, eye).reshape(
        groups, half * 2 * GROUP, half * GROUP
    )
    table_e = np.einsum("gijpa,ik->gaijpk", last, eye).reshape(
        groups, half * GROUP, half * 2 * GROUP
    )
    ang = 2 * math.pi * (np.outer(b, b) % RADIX) / RADIX
    cos, sin = np.cos(ang), np.sin(ang)
    general = np.block([[cos, sin], [-sin, cos]])
    inverse = np.block([[cos, -sin], [sin, cos]])
    hr = RADIX // 2
    packed = np.zeros((2, RADIX, 2, RADIX))
    packed_inv = np.zeros((2, RADIX, 2, RADIX))
    s = np.arange(hr)
    ang0 = 2 * math.pi * (np.outer(s, b) % RADIX) / RADIX
    packed[0, :hr, 0] = np.cos(ang0)
    packed[1, :hr, 0] = -np.sin(ang0)
    packed[1, 0, 0] = (-1.0) ** b
    ang1 = 2 * math.pi * (np.outer(2 * s + 1, b) % (2 * RADIX)) / (2 * RADIX)
    packed[0, hr:, 1] = np.cos(ang1)
    packed[1, hr:, 1] = -np.sin(ang1)
    packed_inv = 2.0 * np.transpose(packed, (2, 3, 0, 1))
    packed_inv[0, :, 0, 0] = 1.0
    packed_inv[0, :, 1, 0] = (-1.0) ** b
    full = 2 * RADIX
    table_b = np.stack([packed.reshape(full, full), general])
    table_c = np.stack([packed_inv.reshape(full, full), inverse])
    return tuple(t.astype(ml_dtypes.bfloat16) for t in (table_a, table_b, table_c, table_e))


def dot(left, right):
    return jnp.dot(left, right, preferred_element_type=F32)


def partner(me, step, count):
    if count & (count - 1):
        return lax.rem(me + step, count)
    peer = me
    bit = 1
    while bit < count:
        if step & bit:
            peer = peer + bit * (1 - 2 * ((me // bit) % 2))
        bit *= 2
    return peer


def send_order(count):
    return sorted(range(1, count), key=lambda k: (-(k // 2).bit_count(), k))


def spectral_product(left, right, conj_left, packed):
    lr = left[:RADIX].astype(F32)
    li = left[RADIX:].astype(F32)
    rr = right[:RADIX].astype(F32)
    ri = right[RADIX:].astype(F32)
    real_real = lr * rr
    imag_imag = li * ri
    if conj_left:
        real = real_real + imag_imag
        imag = lr * ri - li * rr
    else:
        real = real_real - imag_imag
        imag = lr * ri + li * rr
    if packed:
        first = lax.broadcasted_iota(jnp.int32, lr.shape, 0) == 0
        real = jnp.where(first, real_real, real)
        imag = jnp.where(first, imag_imag, imag)
    return jnp.concatenate([real, imag], 0).astype(BF16)


def kernel(
    n_ctx,
    n_dp,
    gin_h,
    val_h,
    gout_h,
    cot_h,
    filt_h,
    ta_h,
    tb_h,
    tc_h,
    te_h,
    gain_h,
    in_out,
    val_out,
    gate_out,
    filt_out,
    gin,
    val,
    gout,
    cot,
    filt,
    ta,
    tb,
    tc,
    te,
    gain,
    mid,
    spec_f,
    mixed,
    mixed_x,
    conv_tok,
    back_tok,
    in_blk,
    val_blk,
    gate_blk,
    parts,
    filt_blk,
    *rest,
):
    me = lax.axis_index("ctx")
    seq = lax.axis_index("dp")
    tok, _ = gin.shape
    length, chans = filt.shape
    halves = max(1, chans // 128)
    lanes = chans // halves
    half = length // RADIX
    groups = RADIX // GROUP
    piece = length // n_dp
    staged, landed, ret, own = (rest[i * halves : (i + 1) * halves] for i in range(4))
    first_sem, load_sem, own_sem, out_sem, send_sem, recv_sem, dp_send, dp_recv = rest[4 * halves :]

    barrier = pltpu.get_barrier_semaphore()
    for k in range(1, n_ctx):
        pl.semaphore_signal(barrier, inc=1, device_id={"ctx": partner(me, k, n_ctx)})
    for k in range(1, n_dp):
        pl.semaphore_signal(barrier, inc=1, device_id={"dp": partner(seq, k, n_dp)})

    def span(start, count, unit):
        return pl.ds(pl.multiple_of(start, unit), count)

    def pair(index):
        return span(index * 2 * lanes, 2 * lanes, 2 * lanes)

    def rows(index, count):
        return span(index * count, count, count)

    def columns(index):
        return span(index * chans, chans, chans)

    order = send_order(n_ctx)

    first_loads = {}
    for k in order + [0]:
        cols = columns(partner(me, k, n_ctx))
        for i, (src, dst) in enumerate(((gin_h, gin), (val_h, val), (cot_h, cot), (gout_h, gout))):
            copy = pltpu.make_async_copy(src.at[:, cols], dst.at[:, cols], first_sem.at[i, k])
            copy.start()
            first_loads[k, i] = copy

    def wait_first(k):
        for i in range(4):
            first_loads[k, i].wait()

    def gate(h, index, target, where):
        cols = span(index * chans + h * lanes, lanes, lanes)
        block = gin[:, cols].astype(F32) * val[:, cols].astype(F32)
        grad = cot[:, cols].astype(F32) * gout[:, cols].astype(F32)
        target[where] = jnp.concatenate([block, grad], 1).astype(BF16)

    def forward_sends(h):
        copies = []
        for k in order:
            peer = partner(me, k, n_ctx)
            if h == 0:
                wait_first(k)
            gate(h, peer, staged[h], (slice(None), pair(peer)))
            copy = pltpu.make_async_remote_copy(
                src_ref=staged[h].at[:, pair(peer)],
                dst_ref=landed[h].at[rows(me, tok), :],
                send_sem=send_sem.at[h, k],
                recv_sem=recv_sem.at[h, k],
                device_id={"ctx": peer},
            )
            copy.start()
            copies.append(copy)
        if h == 0:
            wait_first(0)
        gate(h, me, landed[h], (rows(me, tok), slice(None)))
        return copies

    def return_sends(h):
        copies = {}
        for k in order:
            peer = partner(me, k, n_ctx)
            for t, target in enumerate((conv_tok, back_tok)):
                copy = pltpu.make_async_remote_copy(
                    src_ref=ret[h].at[rows(peer, tok), pl.ds(t * lanes, lanes)],
                    dst_ref=target.at[:, span(me * chans + h * lanes, lanes, lanes)],
                    send_sem=send_sem.at[halves + 2 * h + t, k],
                    recv_sem=recv_sem.at[halves + 2 * h + t, k],
                    device_id={"ctx": peer},
                )
                copy.start()
                copies[k, t] = copy
        return copies

    def part_sends(h):
        copies = []
        for k in range(1, n_dp):
            peer = partner(seq, k, n_dp)
            copy = pltpu.make_async_remote_copy(
                src_ref=own[h].at[rows(peer, piece), :],
                dst_ref=parts.at[h, seq],
                send_sem=dp_send.at[h, k],
                recv_sem=dp_recv.at[h, k],
                device_id={"dp": peer},
            )
            copy.start()
            copies.append(copy)
        return copies

    def finish_parts(h, copies):
        for copy in copies:
            copy.wait_recv()
        total = own[h][rows(seq, piece), :].astype(F32)
        for k in range(1, n_dp):
            total = total + parts[h, partner(seq, k, n_dp)].astype(F32)
        filt_blk[h] = total
        copy = pltpu.make_async_copy(
            filt_blk.at[h], filt_out.at[:, pl.ds(h * lanes, lanes)], own_sem.at[h]
        )
        copy.start()
        return [copy]

    def finish_block(h, k, conv, back):
        cols = span(partner(me, k, n_ctx) * chans + h * lanes, lanes, lanes)
        gain_row = gain[:, cols]
        gin_f = gin[:, cols].astype(F32)
        val_f = val[:, cols].astype(F32)
        cot_f = cot[:, cols].astype(F32)
        gated = (gin_f * val_f).astype(BF16).astype(F32)
        grad = (cot_f * gout[:, cols].astype(F32)).astype(BF16).astype(F32)
        gate_blk[:, cols] = (cot_f * (conv.astype(F32) + gain_row * gated)).astype(BF16)
        grad_gated = back.astype(F32) + gain_row * grad
        in_blk[:, cols] = (grad_gated * val_f).astype(BF16)
        val_blk[:, cols] = (grad_gated * gin_f).astype(BF16)
        copies = []
        for i, (src, dst) in enumerate(
            ((in_blk, in_out), (val_blk, val_out), (gate_blk, gate_out))
        ):
            copy = pltpu.make_async_copy(src.at[:, cols], dst.at[:, cols], out_sem.at[3 * h + i, k])
            copy.start()
            copies.append(copy)
        return copies

    def finish_blocks(h, copies):
        block = ret[h][rows(me, tok), :]
        done = finish_block(h, 0, block[:, :lanes], block[:, lanes:])
        for k in order:
            copies[k, 0].wait_recv()
            copies[k, 1].wait_recv()
            cols = span(partner(me, k, n_ctx) * chans + h * lanes, lanes, lanes)
            done += finish_block(h, k, conv_tok[:, cols], back_tok[:, cols])
        return done

    def repeat(first, count, most, step):
        width = max(w for w in range(1, most + 1) if count % w == 0)

        def body(i, carry):
            stores = [step(first + i * width + u) for u in range(width)]
            for store in stores:
                store()
            return carry

        lax.fori_loop(0, count // width, body, 0)

    def first_stage(source):
        def step(g):
            part = [source[span(a * RADIX + g * GROUP, GROUP, GROUP), :] for a in range(half)]
            out = dot(ta[g], jnp.concatenate(part, 0)).astype(BF16)

            def store():
                for row in range(2 * half):
                    mid[span(row * RADIX + g * GROUP, GROUP, GROUP), : out.shape[1]] = out[
                        row * GROUP : (row + 1) * GROUP
                    ]

            return store

        repeat(0, groups, 4, step)

    def last_stage(source, target):
        def step(g):
            part = [
                source[span(row * RADIX + g * GROUP, GROUP, GROUP), :] for row in range(2 * half)
            ]
            out = dot(te[g], jnp.concatenate(part, 0)).astype(BF16)

            def store():
                for a in range(half):
                    target[span(a * RADIX + g * GROUP, GROUP, GROUP), :] = out[
                        a * GROUP : (a + 1) * GROUP
                    ]

            return store

        repeat(0, groups, 4, step)

    def filter_row(j, packed):
        where = rows(j, 2 * RADIX)
        spec = dot(tb[0 if packed else 1], mid[where, :chans]).astype(BF16)

        def store():
            spec_f[where, :] = spec

        return store

    def half_row(h, j, packed):
        where = rows(j, 2 * RADIX)
        which = 0 if packed else 1
        spec = dot(tb[which], mid[where, :]).astype(BF16)
        spec_g, spec_c = spec[:, :lanes], spec[:, lanes:]
        filt_row = spec_f[where, h * lanes : (h + 1) * lanes]
        cross = spectral_product(spec_g, spec_c, True, packed)
        both = jnp.concatenate(
            [
                spectral_product(filt_row, spec_g, False, packed),
                spectral_product(filt_row, spec_c, True, packed),
            ],
            1,
        )
        out_x = dot(tc[which], cross).astype(BF16)
        out = dot(tc[which], both).astype(BF16)

        def store():
            mixed_x[where, :] = out_x
            mixed[where, :] = out

        return store

    def each_row(step):
        step(0, True)()
        repeat(1, half - 1, 5, lambda j: step(j, False))

    pl.semaphore_wait(barrier, n_ctx - 1 + n_dp - 1)
    sent = [forward_sends(h) for h in range(halves)]

    loads = []
    for i, (src, dst) in enumerate(
        [
            (filt_h, filt),
            (ta_h, ta),
            (tb_h, tb),
            (tc_h, tc),
            (te_h, te),
            (gain_h, gain),
        ]
    ):
        copy = pltpu.make_async_copy(src, dst, load_sem.at[i])
        copy.start()
        loads.append(copy)
    for copy in loads:
        copy.wait()
    first_stage(filt)
    each_row(filter_row)

    parted = []
    returned = []
    for h in range(halves):
        for copy in sent[h]:
            copy.wait_recv()
        first_stage(landed[h])
        each_row(functools.partial(half_row, h))
        last_stage(mixed_x, own[h])
        parted.append(part_sends(h))
        last_stage(mixed, ret[h])
        returned.append(return_sends(h))

    done = []
    for h in range(halves):
        done += finish_parts(h, parted[h])
        done += finish_blocks(h, returned[h])

    for h in range(halves):
        for copy in sent[h] + parted[h] + list(returned[h].values()):
            copy.wait_send()
    for copy in done:
        copy.wait()


def transfer_and_transform(gin, val, gout, cot, filters, gain):
    n_ctx = lax.axis_size("ctx")
    n_dp = lax.axis_size("dp")
    tok, width = gin.shape
    length, chans = filters.shape
    tables = [jnp.asarray(t) for t in make_tables(length)]
    full = 2 * length
    halves = max(1, chans // 128)
    lanes = chans // halves
    pair = 2 * lanes
    piece = length // n_dp
    outs = (jax.ShapeDtypeStruct((tok, width), BF16),) * 3 + (
        jax.ShapeDtypeStruct((piece, chans), F32),
    )
    vmem = lambda *shape: pltpu.VMEM(shape, BF16)
    dma = lambda *shape: pltpu.SemaphoreType.DMA(shape)
    return pl.pallas_call(
        functools.partial(kernel, n_ctx, n_dp),
        out_shape=outs,
        in_specs=[pl.BlockSpec(memory_space=pltpu.HBM)] * 10,
        out_specs=[pl.BlockSpec(memory_space=pl.ANY)] * 4,
        scratch_shapes=[vmem(tok, width)] * 4
        + [vmem(length, chans)]
        + [vmem(*t.shape) for t in tables]
        + [pltpu.VMEM((1, width), F32)]
        + [vmem(full, pair), vmem(full, chans), vmem(full, pair), vmem(full, lanes)]
        + [vmem(tok, width)] * 5
        + [vmem(halves, n_dp, piece, lanes), pltpu.VMEM((halves, piece, lanes), F32)]
        + [vmem(tok, n_ctx * pair)] * halves
        + [vmem(length, pair)] * halves
        + [vmem(length, pair)] * halves
        + [vmem(length, lanes)] * halves
        + [dma(4, n_ctx), dma(6), dma(halves)]
        + [dma(3 * halves, n_ctx)] * 3
        + [dma(halves, n_dp), dma(halves, n_dp)],
        compiler_params=pltpu.CompilerParams(
            collective_id=0, has_side_effects=True, vmem_limit_bytes=52 * 2**20
        ),
        cost_estimate=pl.CostEstimate(
            flops=12 * 2 * 512 * 256 * full * chans // 65536,
            bytes_accessed=12 * 2**20,
            transcendentals=0,
        ),
    )(gin, val, gout, cot, filters, *tables, gain)


def publish_kernel(cuts, *refs):
    count = len(refs) // 2
    sems = refs[-1]
    copies = []
    for i in range(count):
        src, dst = refs[i], refs[count + i]
        size = src.shape[0] // cuts
        for c in range(cuts):
            where = pl.ds(c * size, size)
            copy = pltpu.make_async_copy(src.at[where], dst.at[where], sems.at[i, c])
            copy.start()
            copies.append(copy)
    for copy in copies:
        copy.wait()


def publish(results):
    cuts = 4
    any_spec = pl.BlockSpec(memory_space=pl.ANY)
    size = sum(math.prod(r.shape) * r.dtype.itemsize for r in results)
    return pl.pallas_call(
        functools.partial(publish_kernel, cuts),
        out_shape=tuple(jax.ShapeDtypeStruct(r.shape, r.dtype) for r in results),
        in_specs=[any_spec] * len(results),
        out_specs=[any_spec] * len(results),
        scratch_shapes=[pltpu.SemaphoreType.DMA((len(results), cuts))],
        cost_estimate=pl.CostEstimate(flops=0, bytes_accessed=2 * size, transcendentals=0),
    )(*results)


def on_device(gate_in, values, gate_out, cotangent, filters, skip_gain):
    results = transfer_and_transform(
        gate_in[0], values[0], gate_out[0], cotangent[0], filters, skip_gain[None, :]
    )
    grad_gate_in, grad_values, grad_gate_out, grad_filters = publish(results)
    return (grad_gate_in[None], grad_values[None], grad_gate_out[None], grad_filters)


def solution(mesh):
    return jax.shard_map(
        on_device,
        mesh=mesh,
        in_specs=(
            P("dp", "ctx", None),
            P("dp", "ctx", None),
            P("dp", "ctx", None),
            P("dp", "ctx", None),
            P(None, "ctx"),
            P(),
        ),
        out_specs=(
            P("dp", "ctx", None),
            P("dp", "ctx", None),
            P("dp", "ctx", None),
            P("dp", "ctx"),
        ),
        check_vma=False,
    )
```

```python
import functools
import math

import jax
import jax.numpy as jnp
import ml_dtypes
import numpy as np
from jax import lax
from jax.experimental import pallas as pl
from jax.experimental.pallas import tpu as pltpu
from jax.sharding import PartitionSpec as P

RADIX = 128
GROUP = 16
BF16 = jnp.bfloat16
F32 = jnp.float32


def make_tables(length):
    half = length // RADIX
    size = 2 * length
    scale = length ** (-0.5) / size
    groups = RADIX // GROUP
    a = np.arange(half)
    b = np.arange(RADIX)
    j = np.arange(half)
    pos = 128 * a[None, :] + b[:, None]
    ang = 2 * math.pi * ((pos[:, None, :] * j[None, :, None]) % size) / size
    first = np.stack([np.cos(ang), -np.sin(ang)], 2)
    first[:, 0, 0, :] = 1.0
    first[:, 0, 1, :] = (-1.0) ** a[None, :]
    last = first * np.where(j == 0, scale, 2 * scale)[None, :, None, None]
    first = first.reshape(groups, GROUP, half, 2, half)
    last = last.reshape(groups, GROUP, half, 2, half)
    eye = np.eye(GROUP)
    table_a = np.einsum("gijpa,ik->gjpiak", first, eye).reshape(
        groups, half * 2 * GROUP, half * GROUP
    )
    table_e = np.einsum("gijpa,ik->gaijpk", last, eye).reshape(
        groups, half * GROUP, half * 2 * GROUP
    )
    ang = 2 * math.pi * (np.outer(b, b) % RADIX) / RADIX
    cos, sin = np.cos(ang), np.sin(ang)
    general = np.block([[cos, sin], [-sin, cos]])
    inverse = np.block([[cos, -sin], [sin, cos]])
    hr = RADIX // 2
    packed = np.zeros((2, RADIX, 2, RADIX))
    packed_inv = np.zeros((2, RADIX, 2, RADIX))
    s = np.arange(hr)
    ang0 = 2 * math.pi * (np.outer(s, b) % RADIX) / RADIX
    packed[0, :hr, 0] = np.cos(ang0)
    packed[1, :hr, 0] = -np.sin(ang0)
    packed[1, 0, 0] = (-1.0) ** b
    ang1 = 2 * math.pi * (np.outer(2 * s + 1, b) % (2 * RADIX)) / (2 * RADIX)
    packed[0, hr:, 1] = np.cos(ang1)
    packed[1, hr:, 1] = -np.sin(ang1)
    packed_inv = 2.0 * np.transpose(packed, (2, 3, 0, 1))
    packed_inv[0, :, 0, 0] = 1.0
    packed_inv[0, :, 1, 0] = (-1.0) ** b
    full = 2 * RADIX
    table_b = np.concatenate([packed.reshape(full, full), general], 1)
    table_c = np.concatenate([packed_inv.reshape(full, full), inverse], 1)
    wide = table_e.shape[2]
    joined = np.concatenate(
        [np.pad(t, ((0, 0), (0, wide - 2 * full))) for t in (table_b, table_c)]
        + [table_e.reshape(-1, wide)]
    )
    return tuple(t.astype(ml_dtypes.bfloat16) for t in (table_a, joined))


def dot(left, right):
    return jnp.dot(left, right, preferred_element_type=F32)


def partner(me, step, count):
    if count & (count - 1):
        return lax.rem(me + step, count)
    peer = me
    bit = 1
    while bit < count:
        if step & bit:
            peer = peer + bit * (1 - 2 * ((me // bit) % 2))
        bit *= 2
    return peer


def send_order(count):
    return sorted(range(1, count), key=lambda k: (-(k // 2).bit_count(), k))


def spectral_product(left, right, conj_left, packed):
    lr = left[:RADIX].astype(F32)
    li = left[RADIX:].astype(F32)
    rr = right[:RADIX].astype(F32)
    ri = right[RADIX:].astype(F32)
    real_real = lr * rr
    imag_imag = li * ri
    if conj_left:
        real = real_real + imag_imag
        imag = lr * ri - li * rr
    else:
        real = real_real - imag_imag
        imag = lr * ri + li * rr
    if packed:
        first = lax.broadcasted_iota(jnp.int32, lr.shape, 0) == 0
        real = jnp.where(first, real_real, real)
        imag = jnp.where(first, imag_imag, imag)
    return jnp.concatenate([real, imag], 0).astype(BF16)


def kernel(
    n_ctx,
    n_dp,
    gin_h,
    val_h,
    gout_h,
    cot_h,
    filt_h,
    ta_h,
    te_h,
    gain_h,
    in_out,
    val_out,
    gate_out,
    filt_out,
    gin,
    val,
    gout,
    cot,
    filt,
    ta,
    te,
    gain,
    mid,
    spec_f,
    mixed,
    mixed_x,
    conv_tok,
    back_tok,
    parts,
    *rest,
):
    me = lax.axis_index("ctx")
    seq = lax.axis_index("dp")
    tok, _ = gin.shape
    length, chans = filt.shape
    halves = max(1, chans // 128)
    lanes = chans // halves
    half = length // RADIX
    groups = RADIX // GROUP
    piece = length // n_dp
    staged, landed, ret, own = (rest[i * halves : (i + 1) * halves] for i in range(4))
    first_sem, load_sem, send_sem, recv_sem, dp_send, dp_recv = rest[4 * halves :]

    barrier = pltpu.get_barrier_semaphore()
    for k in range(1, n_ctx):
        pl.semaphore_signal(barrier, inc=1, device_id={"ctx": partner(me, k, n_ctx)})
    for k in range(1, n_dp):
        pl.semaphore_signal(barrier, inc=1, device_id={"dp": partner(seq, k, n_dp)})

    def span(start, count, unit):
        return pl.ds(pl.multiple_of(start, unit), count)

    def pair(index):
        return span(index * 2 * lanes, 2 * lanes, 2 * lanes)

    def rows(index, count):
        return span(index * count, count, count)

    def columns(index):
        return span(index * chans, chans, chans)

    order = send_order(n_ctx)

    first_loads = {}
    for k in order + [0]:
        cols = columns(partner(me, k, n_ctx))
        for i, (src, dst) in enumerate(((gin_h, gin), (val_h, val), (cot_h, cot), (gout_h, gout))):
            copy = pltpu.make_async_copy(src.at[:, cols], dst.at[:, cols], first_sem.at[i, k])
            copy.start()
            first_loads[k, i] = copy

    def wait_first(k):
        for i in range(4):
            first_loads[k, i].wait()

    def gate(h, index, target, where):
        cols = span(index * chans + h * lanes, lanes, lanes)
        block = gin[:, cols].astype(F32) * val[:, cols].astype(F32)
        grad = cot[:, cols].astype(F32) * gout[:, cols].astype(F32)
        target[where] = jnp.concatenate([block, grad], 1).astype(BF16)

    def forward_sends(h):
        copies = []
        for k in order:
            peer = partner(me, k, n_ctx)
            if h == 0:
                wait_first(k)
            gate(h, peer, staged[h], (slice(None), pair(peer)))
            copy = pltpu.make_async_remote_copy(
                src_ref=staged[h].at[:, pair(peer)],
                dst_ref=landed[h].at[rows(me, tok), :],
                send_sem=send_sem.at[h, k],
                recv_sem=recv_sem.at[h, k],
                device_id={"ctx": peer},
            )
            copy.start()
            copies.append(copy)
        if h == 0:
            wait_first(0)
        gate(h, me, landed[h], (rows(me, tok), slice(None)))
        return copies

    def return_sends(h):
        copies = {}
        for k in order:
            peer = partner(me, k, n_ctx)
            for t, target in enumerate((conv_tok, back_tok)):
                copy = pltpu.make_async_remote_copy(
                    src_ref=ret[h].at[rows(peer, tok), pl.ds(t * lanes, lanes)],
                    dst_ref=target.at[:, span(me * chans + h * lanes, lanes, lanes)],
                    send_sem=send_sem.at[halves + 2 * h + t, k],
                    recv_sem=recv_sem.at[halves + 2 * h + t, k],
                    device_id={"ctx": peer},
                )
                copy.start()
                copies[k, t] = copy
        return copies

    def part_sends(h):
        copies = []
        for k in range(1, n_dp):
            peer = partner(seq, k, n_dp)
            copy = pltpu.make_async_remote_copy(
                src_ref=own[h].at[rows(peer, piece), :],
                dst_ref=parts.at[h, seq],
                send_sem=dp_send.at[h, k],
                recv_sem=dp_recv.at[h, k],
                device_id={"dp": peer},
            )
            copy.start()
            copies.append(copy)
        return copies

    def finish_parts(h, copies):
        for copy in copies:
            copy.wait_recv()
        total = own[h][rows(seq, piece), :].astype(F32)
        for k in range(1, n_dp):
            total = total + parts[h, partner(seq, k, n_dp)].astype(F32)
        filt_out[:, h * lanes : (h + 1) * lanes] = total

    def finish_block(h, k, conv, back):
        cols = span(partner(me, k, n_ctx) * chans + h * lanes, lanes, lanes)
        gain_row = gain[:, cols]
        gin_f = gin[:, cols].astype(F32)
        val_f = val[:, cols].astype(F32)
        cot_f = cot[:, cols].astype(F32)
        gated = (gin_f * val_f).astype(BF16).astype(F32)
        grad = (cot_f * gout[:, cols].astype(F32)).astype(BF16).astype(F32)
        gate_out[:, cols] = (cot_f * (conv.astype(F32) + gain_row * gated)).astype(BF16)
        grad_gated = back.astype(F32) + gain_row * grad
        in_out[:, cols] = (grad_gated * val_f).astype(BF16)
        val_out[:, cols] = (grad_gated * gin_f).astype(BF16)

    def finish_blocks(h, copies):
        block = ret[h][rows(me, tok), :]
        finish_block(h, 0, block[:, :lanes], block[:, lanes:])
        for k in order:
            copies[k, 0].wait_recv()
            copies[k, 1].wait_recv()
            cols = span(partner(me, k, n_ctx) * chans + h * lanes, lanes, lanes)
            finish_block(h, k, conv_tok[:, cols], back_tok[:, cols])

    def repeat(first, count, most, step):
        width = max(w for w in range(1, most + 1) if count % w == 0)

        def body(i, carry):
            stores = [step(first + i * width + u) for u in range(width)]
            for store in stores:
                store()
            return carry

        lax.fori_loop(0, count // width, body, 0)

    def first_stage(source):
        def step(g):
            part = [source[span(a * RADIX + g * GROUP, GROUP, GROUP), :] for a in range(half)]
            out = dot(ta[g], jnp.concatenate(part, 0)).astype(BF16)

            def store():
                for row in range(2 * half):
                    mid[span(row * RADIX + g * GROUP, GROUP, GROUP), : out.shape[1]] = out[
                        row * GROUP : (row + 1) * GROUP
                    ]

            return store

        repeat(0, groups, 4, step)

    def last_stage(source, target):
        def step(g):
            part = [
                source[span(row * RADIX + g * GROUP, GROUP, GROUP), :] for row in range(2 * half)
            ]
            out = dot(te[span(4 * RADIX + g * half * GROUP, half * GROUP, GROUP), :], jnp.concatenate(part, 0)).astype(BF16)

            def store():
                for a in range(half):
                    target[span(a * RADIX + g * GROUP, GROUP, GROUP), :] = out[
                        a * GROUP : (a + 1) * GROUP
                    ]

            return store

        repeat(0, groups, 4, step)

    def second(which, packed):
        col = 0 if packed else 2 * RADIX
        return te[pl.ds(which * 2 * RADIX, 2 * RADIX), pl.ds(col, 2 * RADIX)]

    def filter_row(j, packed):
        where = rows(j, 2 * RADIX)
        spec = dot(second(0, packed), mid[where, :chans]).astype(BF16)

        def store():
            spec_f[where, :] = spec

        return store

    def half_row(h, j, packed):
        where = rows(j, 2 * RADIX)
        spec = dot(second(0, packed), mid[where, :]).astype(BF16)
        spec_g, spec_c = spec[:, :lanes], spec[:, lanes:]
        filt_row = spec_f[where, h * lanes : (h + 1) * lanes]
        cross = spectral_product(spec_g, spec_c, True, packed)
        both = jnp.concatenate(
            [
                spectral_product(filt_row, spec_g, False, packed),
                spectral_product(filt_row, spec_c, True, packed),
            ],
            1,
        )
        out_x = dot(second(1, packed), cross).astype(BF16)
        out = dot(second(1, packed), both).astype(BF16)

        def store():
            mixed_x[where, :] = out_x
            mixed[where, :] = out

        return store

    def each_row(step):
        step(0, True)()
        repeat(1, half - 1, 5, lambda j: step(j, False))

    pl.semaphore_wait(barrier, n_ctx - 1 + n_dp - 1)
    sent = [forward_sends(h) for h in range(halves)]

    loads = []
    for i, (src, dst) in enumerate(
        [
            (filt_h, filt),
            (ta_h, ta),
            (te_h, te),
            (gain_h, gain),
        ]
    ):
        copy = pltpu.make_async_copy(src, dst, load_sem.at[i])
        copy.start()
        loads.append(copy)
    for copy in loads:
        copy.wait()
    first_stage(filt)
    each_row(filter_row)

    parted = []
    returned = []
    for h in range(halves):
        for copy in sent[h]:
            copy.wait_recv()
        first_stage(landed[h])
        each_row(functools.partial(half_row, h))
        if h == halves - 1:
            last_stage(mixed_x, own[h])
            parted.append(part_sends(h))
        last_stage(mixed, ret[h])
        returned.append(return_sends(h))
        if h < halves - 1:
            last_stage(mixed_x, own[h])
            parted.append(part_sends(h))

    for h in range(halves):
        finish_parts(h, parted[h])
        finish_blocks(h, returned[h])

    for h in range(halves):
        for copy in sent[h] + parted[h] + list(returned[h].values()):
            copy.wait_send()


def transfer_and_transform(gin, val, gout, cot, filters, gain):
    n_ctx = lax.axis_size("ctx")
    n_dp = lax.axis_size("dp")
    tok, width = gin.shape
    length, chans = filters.shape
    tables = [jnp.asarray(t) for t in make_tables(length)]
    full = 2 * length
    halves = max(1, chans // 128)
    lanes = chans // halves
    pair = 2 * lanes
    piece = length // n_dp
    outs = (pltpu.VMEM((tok, width), BF16),) * 3 + (pltpu.VMEM((piece, chans), F32),)
    vmem = lambda *shape: pltpu.VMEM(shape, BF16)
    dma = lambda *shape: pltpu.SemaphoreType.DMA(shape)
    return pl.pallas_call(
        functools.partial(kernel, n_ctx, n_dp),
        out_shape=outs,
        in_specs=[pl.BlockSpec(memory_space=pltpu.HBM)] * 8,
        out_specs=[pl.BlockSpec(memory_space=pltpu.VMEM)] * 4,
        scratch_shapes=[vmem(tok, width)] * 4
        + [vmem(length, chans)]
        + [vmem(*t.shape) for t in tables]
        + [pltpu.VMEM((1, width), F32)]
        + [vmem(full, pair), vmem(full, chans), vmem(full, pair), vmem(full, lanes)]
        + [vmem(tok, width)] * 2
        + [vmem(halves, n_dp, piece, lanes)]
        + [vmem(tok, n_ctx * pair)] * halves
        + [vmem(length, pair)] * halves
        + [vmem(length, pair)] * halves
        + [vmem(length, lanes)] * halves
        + [dma(4, n_ctx), dma(4)]
        + [dma(3 * halves, n_ctx)] * 2
        + [dma(halves, n_dp), dma(halves, n_dp)],
        compiler_params=pltpu.CompilerParams(
            collective_id=0, has_side_effects=True, vmem_limit_bytes=56 * 2**20
        ),
        cost_estimate=pl.CostEstimate(
            flops=12 * 2 * 512 * 256 * full * chans // 65536,
            bytes_accessed=12 * 2**20,
            transcendentals=0,
        ),
    )(gin, val, gout, cot, filters, *tables, gain)


def publish_kernel(cuts, *refs):
    count = len(refs) // 2
    sems = refs[-1]
    copies = []
    for i in range(count):
        src, dst = refs[i], refs[count + i]
        size = src.shape[0] // cuts
        for c in range(cuts):
            where = pl.ds(c * size, size)
            copy = pltpu.make_async_copy(src.at[where], dst.at[where], sems.at[i, c])
            copy.start()
            copies.append(copy)
    for copy in copies:
        copy.wait()


def publish(results):
    cuts = 4
    any_spec = pl.BlockSpec(memory_space=pl.ANY)
    size = sum(math.prod(r.shape) * r.dtype.itemsize for r in results)
    return pl.pallas_call(
        functools.partial(publish_kernel, cuts),
        out_shape=tuple(jax.ShapeDtypeStruct(r.shape, r.dtype) for r in results),
        in_specs=[pl.BlockSpec(memory_space=pltpu.VMEM)] * len(results),
        out_specs=[any_spec] * len(results),
        scratch_shapes=[pltpu.SemaphoreType.DMA((len(results), cuts))],
        cost_estimate=pl.CostEstimate(flops=0, bytes_accessed=2 * size, transcendentals=0),
    )(*results)


def on_device(gate_in, values, gate_out, cotangent, filters, skip_gain):
    results = transfer_and_transform(
        gate_in[0], values[0], gate_out[0], cotangent[0], filters, skip_gain[None, :]
    )
    grad_gate_in, grad_values, grad_gate_out, grad_filters = publish(results)
    return (grad_gate_in[None], grad_values[None], grad_gate_out[None], grad_filters)


def solution(mesh):
    return jax.shard_map(
        on_device,
        mesh=mesh,
        in_specs=(
            P("dp", "ctx", None),
            P("dp", "ctx", None),
            P("dp", "ctx", None),
            P("dp", "ctx", None),
            P(None, "ctx"),
            P(),
        ),
        out_specs=(
            P("dp", "ctx", None),
            P("dp", "ctx", None),
            P("dp", "ctx", None),
            P("dp", "ctx"),
        ),
        check_vma=False,
    )
```

```python
import functools
import math

import jax
import jax.numpy as jnp
import ml_dtypes
import numpy as np
from jax import lax
from jax.experimental import pallas as pl
from jax.experimental.pallas import tpu as pltpu
from jax.sharding import PartitionSpec as P

RADIX = 128
GROUP = 16
BF16 = jnp.bfloat16
F32 = jnp.float32


def make_tables(length):
    half = length // RADIX
    size = 2 * length
    scale = length ** (-0.5) / size
    groups = RADIX // GROUP
    a = np.arange(half)
    b = np.arange(RADIX)
    j = np.arange(half)
    pos = 128 * a[None, :] + b[:, None]
    ang = 2 * math.pi * ((pos[:, None, :] * j[None, :, None]) % size) / size
    first = np.stack([np.cos(ang), -np.sin(ang)], 2)
    first[:, 0, 0, :] = 1.0
    first[:, 0, 1, :] = (-1.0) ** a[None, :]
    last = first * np.where(j == 0, scale, 2 * scale)[None, :, None, None]
    first = first.reshape(groups, GROUP, half, 2, half)
    last = last.reshape(groups, GROUP, half, 2, half)
    eye = np.eye(GROUP)
    table_a = np.einsum("gijpa,ik->gjpiak", first, eye).reshape(
        groups, half * 2 * GROUP, half * GROUP
    )
    table_e = np.einsum("gijpa,ik->gaijpk", last, eye).reshape(
        groups, half * GROUP, half * 2 * GROUP
    )
    ang = 2 * math.pi * (np.outer(b, b) % RADIX) / RADIX
    cos, sin = np.cos(ang), np.sin(ang)
    general = np.block([[cos, sin], [-sin, cos]])
    inverse = np.block([[cos, -sin], [sin, cos]])
    hr = RADIX // 2
    packed = np.zeros((2, RADIX, 2, RADIX))
    packed_inv = np.zeros((2, RADIX, 2, RADIX))
    s = np.arange(hr)
    ang0 = 2 * math.pi * (np.outer(s, b) % RADIX) / RADIX
    packed[0, :hr, 0] = np.cos(ang0)
    packed[1, :hr, 0] = -np.sin(ang0)
    packed[1, 0, 0] = (-1.0) ** b
    ang1 = 2 * math.pi * (np.outer(2 * s + 1, b) % (2 * RADIX)) / (2 * RADIX)
    packed[0, hr:, 1] = np.cos(ang1)
    packed[1, hr:, 1] = -np.sin(ang1)
    packed_inv = 2.0 * np.transpose(packed, (2, 3, 0, 1))
    packed_inv[0, :, 0, 0] = 1.0
    packed_inv[0, :, 1, 0] = (-1.0) ** b
    full = 2 * RADIX
    table_b = np.concatenate([packed.reshape(full, full), general], 1)
    table_c = np.concatenate([packed_inv.reshape(full, full), inverse], 1)
    wide = table_e.shape[2]
    joined = np.concatenate(
        [np.pad(t, ((0, 0), (0, wide - 2 * full))) for t in (table_b, table_c)]
        + [table_e.reshape(-1, wide)]
    )
    return tuple(t.astype(ml_dtypes.bfloat16) for t in (table_a, joined))


def dot(left, right):
    return jnp.dot(left, right, preferred_element_type=F32)


def partner(me, step, count):
    if count & (count - 1):
        return lax.rem(me + step, count)
    peer = me
    bit = 1
    while bit < count:
        if step & bit:
            peer = peer + bit * (1 - 2 * ((me // bit) % 2))
        bit *= 2
    return peer


def send_order(count):
    return sorted(range(1, count), key=lambda k: (-(k // 2).bit_count(), k))


def spectral_product(left, right, conj_left, packed):
    lr = left[:RADIX].astype(F32)
    li = left[RADIX:].astype(F32)
    rr = right[:RADIX].astype(F32)
    ri = right[RADIX:].astype(F32)
    real_real = lr * rr
    imag_imag = li * ri
    if conj_left:
        real = real_real + imag_imag
        imag = lr * ri - li * rr
    else:
        real = real_real - imag_imag
        imag = lr * ri + li * rr
    if packed:
        first = lax.broadcasted_iota(jnp.int32, lr.shape, 0) == 0
        real = jnp.where(first, real_real, real)
        imag = jnp.where(first, imag_imag, imag)
    return jnp.concatenate([real, imag], 0).astype(BF16)


def kernel(
    n_ctx,
    n_dp,
    gin_h,
    val_h,
    gout_h,
    cot_h,
    filt_h,
    ta_h,
    te_h,
    gain_h,
    in_out,
    val_out,
    gate_out,
    filt_out,
    gin,
    val,
    gout,
    cot,
    filt,
    ta,
    te,
    gain,
    mid,
    spec_f,
    mixed,
    mixed_x,
    conv_tok,
    back_tok,
    parts,
    *rest,
):
    me = lax.axis_index("ctx")
    seq = lax.axis_index("dp")
    tok, _ = gin.shape
    length, chans = filt.shape
    halves = max(1, chans // 128)
    lanes = chans // halves
    half = length // RADIX
    groups = RADIX // GROUP
    piece = length // n_dp
    staged, landed, ret, own = (rest[i * halves : (i + 1) * halves] for i in range(4))
    first_sem, load_sem, send_sem, recv_sem, dp_send, dp_recv = rest[4 * halves :]

    barrier = pltpu.get_barrier_semaphore()
    for k in range(1, n_ctx):
        pl.semaphore_signal(barrier, inc=1, device_id={"ctx": partner(me, k, n_ctx)})
    for k in range(1, n_dp):
        pl.semaphore_signal(barrier, inc=1, device_id={"dp": partner(seq, k, n_dp)})

    def span(start, count, unit):
        return pl.ds(pl.multiple_of(start, unit), count)

    def pair(index):
        return span(index * 2 * lanes, 2 * lanes, 2 * lanes)

    def rows(index, count):
        return span(index * count, count, count)

    def columns(index):
        return span(index * chans, chans, chans)

    order = send_order(n_ctx)

    first_loads = {}
    for k in order + [0]:
        cols = columns(partner(me, k, n_ctx))
        for i, (src, dst) in enumerate(((gin_h, gin), (val_h, val), (cot_h, cot), (gout_h, gout))):
            copy = pltpu.make_async_copy(src.at[:, cols], dst.at[:, cols], first_sem.at[i, k])
            copy.start()
            first_loads[k, i] = copy

    def wait_first(k):
        for i in range(4):
            first_loads[k, i].wait()

    def gate(h, index, target, where):
        cols = span(index * chans + h * lanes, lanes, lanes)
        block = gin[:, cols].astype(F32) * val[:, cols].astype(F32)
        grad = cot[:, cols].astype(F32) * gout[:, cols].astype(F32)
        target[where] = jnp.concatenate([block, grad], 1).astype(BF16)

    def forward_sends(h):
        copies = []
        for k in order:
            peer = partner(me, k, n_ctx)
            if h == 0:
                wait_first(k)
            gate(h, peer, staged[h], (slice(None), pair(peer)))
            copy = pltpu.make_async_remote_copy(
                src_ref=staged[h].at[:, pair(peer)],
                dst_ref=landed[h].at[rows(me, tok), :],
                send_sem=send_sem.at[h, k],
                recv_sem=recv_sem.at[h, k],
                device_id={"ctx": peer},
            )
            copy.start()
            copies.append(copy)
        if h == 0:
            wait_first(0)
        gate(h, me, landed[h], (rows(me, tok), slice(None)))
        return copies

    def return_sends(h):
        copies = {}
        for k in order:
            peer = partner(me, k, n_ctx)
            for t, target in enumerate((conv_tok, back_tok)):
                copy = pltpu.make_async_remote_copy(
                    src_ref=ret[h].at[rows(peer, tok), pl.ds(t * lanes, lanes)],
                    dst_ref=target.at[:, span(me * chans + h * lanes, lanes, lanes)],
                    send_sem=send_sem.at[halves + 2 * h + t, k],
                    recv_sem=recv_sem.at[halves + 2 * h + t, k],
                    device_id={"ctx": peer},
                )
                copy.start()
                copies[k, t] = copy
        return copies

    def part_sends(h):
        copies = []
        for k in range(1, n_dp):
            peer = partner(seq, k, n_dp)
            copy = pltpu.make_async_remote_copy(
                src_ref=own[h].at[rows(peer, piece), :],
                dst_ref=parts.at[h, seq],
                send_sem=dp_send.at[h, k],
                recv_sem=dp_recv.at[h, k],
                device_id={"dp": peer},
            )
            copy.start()
            copies.append(copy)
        return copies

    def finish_parts(h, copies):
        for copy in copies:
            copy.wait_recv()
        total = own[h][rows(seq, piece), :].astype(F32)
        for k in range(1, n_dp):
            total = total + parts[h, partner(seq, k, n_dp)].astype(F32)
        filt_out[:, h * lanes : (h + 1) * lanes] = total

    def finish_block(h, k, conv, back):
        cols = span(partner(me, k, n_ctx) * chans + h * lanes, lanes, lanes)
        gain_row = gain[:, cols]
        gin_f = gin[:, cols].astype(F32)
        val_f = val[:, cols].astype(F32)
        cot_f = cot[:, cols].astype(F32)
        gated = (gin_f * val_f).astype(BF16).astype(F32)
        grad = (cot_f * gout[:, cols].astype(F32)).astype(BF16).astype(F32)
        gate_out[:, cols] = (cot_f * (conv.astype(F32) + gain_row * gated)).astype(BF16)
        grad_gated = back.astype(F32) + gain_row * grad
        in_out[:, cols] = (grad_gated * val_f).astype(BF16)
        val_out[:, cols] = (grad_gated * gin_f).astype(BF16)

    def finish_blocks(h, copies):
        block = ret[h][rows(me, tok), :]
        finish_block(h, 0, block[:, :lanes], block[:, lanes:])
        for k in order:
            copies[k, 0].wait_recv()
            copies[k, 1].wait_recv()
            cols = span(partner(me, k, n_ctx) * chans + h * lanes, lanes, lanes)
            finish_block(h, k, conv_tok[:, cols], back_tok[:, cols])

    def repeat(first, count, most, step):
        width = max(w for w in range(1, most + 1) if count % w == 0)

        def body(i, carry):
            stores = [step(first + i * width + u) for u in range(width)]
            for store in stores:
                store()
            return carry

        lax.fori_loop(0, count // width, body, 0)

    def first_stage(source):
        def step(g):
            part = [source[span(a * RADIX + g * GROUP, GROUP, GROUP), :] for a in range(half)]
            out = dot(ta[g], jnp.concatenate(part, 0)).astype(BF16)

            def store():
                for row in range(2 * half):
                    mid[span(row * RADIX + g * GROUP, GROUP, GROUP), : out.shape[1]] = out[
                        row * GROUP : (row + 1) * GROUP
                    ]

            return store

        repeat(0, groups, 4, step)

    def last_stage(source, target):
        def step(g):
            part = [
                source[span(row * RADIX + g * GROUP, GROUP, GROUP), :] for row in range(2 * half)
            ]
            out = dot(te[span(4 * RADIX + g * half * GROUP, half * GROUP, GROUP), :], jnp.concatenate(part, 0)).astype(BF16)

            def store():
                for a in range(half):
                    target[span(a * RADIX + g * GROUP, GROUP, GROUP), :] = out[
                        a * GROUP : (a + 1) * GROUP
                    ]

            return store

        repeat(0, groups, 4, step)

    def second(which, packed):
        col = 0 if packed else 2 * RADIX
        return te[pl.ds(which * 2 * RADIX, 2 * RADIX), pl.ds(col, 2 * RADIX)]

    def filter_row(j, packed):
        where = rows(j, 2 * RADIX)
        spec = dot(second(0, packed), mid[where, :chans]).astype(BF16)

        def store():
            spec_f[where, :] = spec

        return store

    def half_row(h, j, packed):
        where = rows(j, 2 * RADIX)
        spec = dot(second(0, packed), mid[where, :]).astype(BF16)
        spec_g, spec_c = spec[:, :lanes], spec[:, lanes:]
        filt_row = spec_f[where, h * lanes : (h + 1) * lanes]
        cross = spectral_product(spec_g, spec_c, True, packed)
        both = jnp.concatenate(
            [
                spectral_product(filt_row, spec_g, False, packed),
                spectral_product(filt_row, spec_c, True, packed),
            ],
            1,
        )
        out_x = dot(second(1, packed), cross).astype(BF16)
        out = dot(second(1, packed), both).astype(BF16)

        def store():
            mixed_x[where, :] = out_x
            mixed[where, :] = out

        return store

    def each_row(step):
        step(0, True)()
        repeat(1, half - 1, 5, lambda j: step(j, False))

    pl.semaphore_wait(barrier, n_ctx - 1 + n_dp - 1)
    sent = [forward_sends(h) for h in range(halves)]

    loads = []
    for i, (src, dst) in enumerate(
        [
            (filt_h, filt),
            (ta_h, ta),
            (te_h, te),
            (gain_h, gain),
        ]
    ):
        copy = pltpu.make_async_copy(src, dst, load_sem.at[i])
        copy.start()
        loads.append(copy)
    for copy in loads:
        copy.wait()
    first_stage(filt)
    each_row(filter_row)

    parted = []
    returned = []
    for h in range(halves):
        for copy in sent[h]:
            copy.wait_recv()
        first_stage(landed[h])
        each_row(functools.partial(half_row, h))
        if h == halves - 1:
            last_stage(mixed_x, own[h])
            parted.append(part_sends(h))
        last_stage(mixed, ret[h])
        returned.append(return_sends(h))
        if h < halves - 1:
            last_stage(mixed_x, own[h])
            parted.append(part_sends(h))

    for h in range(halves):
        finish_parts(h, parted[h])
        finish_blocks(h, returned[h])

    for h in range(halves):
        for copy in sent[h] + parted[h] + list(returned[h].values()):
            copy.wait_send()


def transfer_and_transform(gin, val, gout, cot, filters, gain):
    n_ctx = lax.axis_size("ctx")
    n_dp = lax.axis_size("dp")
    tok, width = gin.shape
    length, chans = filters.shape
    tables = [jnp.asarray(t) for t in make_tables(length)]
    full = 2 * length
    halves = max(1, chans // 128)
    lanes = chans // halves
    pair = 2 * lanes
    piece = length // n_dp
    outs = (pltpu.VMEM((tok, width), BF16),) * 3 + (pltpu.VMEM((piece, chans), F32),)
    vmem = lambda *shape: pltpu.VMEM(shape, BF16)
    dma = lambda *shape: pltpu.SemaphoreType.DMA(shape)
    return pl.pallas_call(
        functools.partial(kernel, n_ctx, n_dp),
        out_shape=outs,
        in_specs=[pl.BlockSpec(memory_space=pltpu.HBM)] * 8,
        out_specs=[pl.BlockSpec(memory_space=pltpu.VMEM)] * 4,
        scratch_shapes=[vmem(tok, width)] * 4
        + [vmem(length, chans)]
        + [vmem(*t.shape) for t in tables]
        + [pltpu.VMEM((1, width), F32)]
        + [vmem(full, pair), vmem(full, chans), vmem(full, pair), vmem(full, lanes)]
        + [vmem(tok, width)] * 2
        + [vmem(halves, n_dp, piece, lanes)]
        + [vmem(tok, n_ctx * pair)] * halves
        + [vmem(length, pair)] * halves
        + [vmem(length, pair)] * halves
        + [vmem(length, lanes)] * halves
        + [dma(4, n_ctx), dma(4)]
        + [dma(3 * halves, n_ctx)] * 2
        + [dma(halves, n_dp), dma(halves, n_dp)],
        compiler_params=pltpu.CompilerParams(
            collective_id=0, has_side_effects=True, vmem_limit_bytes=56 * 2**20
        ),
        cost_estimate=pl.CostEstimate(
            flops=12 * 2 * 512 * 256 * full * chans // 65536,
            bytes_accessed=12 * 2**20,
            transcendentals=0,
        ),
    )(gin, val, gout, cot, filters, *tables, gain)


def on_device(gate_in, values, gate_out, cotangent, filters, skip_gain):
    grad_gate_in, grad_values, grad_gate_out, grad_filters = transfer_and_transform(
        gate_in[0], values[0], gate_out[0], cotangent[0], filters, skip_gain[None, :]
    )
    return (grad_gate_in[None], grad_values[None], grad_gate_out[None], grad_filters)


def solution(mesh):
    return jax.shard_map(
        on_device,
        mesh=mesh,
        in_specs=(
            P("dp", "ctx", None),
            P("dp", "ctx", None),
            P("dp", "ctx", None),
            P("dp", "ctx", None),
            P(None, "ctx"),
            P(),
        ),
        out_specs=(
            P("dp", "ctx", None),
            P("dp", "ctx", None),
            P("dp", "ctx", None),
            P("dp", "ctx"),
        ),
        check_vma=False,
    )
```
